32 devices in a mesh: visit: 8 (over z, x), patch: 4 (over y, core).
Axes of the slice: x: 2, y: 2, z: 4, core: 2. Of those that a mesh axis runs over, the one named last changes fastest.
Arguments:
- templates: float32 [8, 2, 64, 1024], P('visit', None, 'patch'), may hold values from -16 to 16, as said below
- owners: int32 [2], replicated, may hold values from 0 to 7, as said below
- science: float32 [2, 8, 64, 1024], P(None, 'visit', 'patch'), may hold values from -40 to 40
- sci_var: float32 [2, 8, 64, 1024], P(None, 'visit', 'patch'), may hold values from 0.03 to 0.3
- bad_pixels: int32 [2, 8, 64, 1024], P(None, 'visit', 'patch'), may hold values 0 or 1
Outputs:
- significance: float32 [2, 8, 64, 1024], P(None, 'visit', 'patch')
The draws below stay inside these ranges and needn't reach their ends.
Inputs may be any that keep to these rules, and one draw needn't show every extreme that they name: `owners`: the steps' entries are distinct indices of stored tiles, one of them always 8 - 1. `templates`: variances (index 1) lie in 0.01 to 0.1.
All inputs are finite; a program needn't handle non-finite values. No bound on the sum of `bad_pixels` on one device may be relied on, other than what follows from the above.
Results may differ from the reference program's by a relative error of at most 0.0003.
Values sent between devices are 32-bit elements; how exact they have to be, the bound alone decides.
No kernel may reach another device: no remote copies, remote signals or barrier semaphores. Data moves between devices by JAX's collectives and lax.ppermute only.
A program may use at most 64 MiB of HBM per device.

```python
import math
import jax
import jax.numpy as jnp
import numpy as np
from jax import lax

COLS = 1024
NPROF = 5
RAD = 10
STEPS = 2
ROWS = 64
VISITS = 8
TEMPLATES = 8


def template_stack(key):
    image_key, var_key = jax.random.split(jax.random.fold_in(key, 11))
    position = jnp.arange(ROWS).astype(jnp.float32) / ROWS
    row_scale = jnp.exp(position * math.log(3.0))
    image = jax.random.truncated_normal(image_key, -4.0, 4.0, (TEMPLATES, ROWS, COLS), jnp.float32) * row_scale[None, :, None]
    variance = jnp.exp(jax.random.uniform(var_key, (TEMPLATES, ROWS, COLS), jnp.float32, math.log(0.01), math.log(0.1)))
    return jnp.stack([image, variance], axis=1)


def owner_list(key):
    first_key, order_key = jax.random.split(jax.random.fold_in(key, 23))
    chosen = jax.random.permutation(first_key, TEMPLATES - 1)[:STEPS - 1]
    listed = jnp.concatenate([chosen.astype(jnp.int32), jnp.full((1,), TEMPLATES - 1, jnp.int32)])
    order = jax.random.permutation(order_key, STEPS)
    return listed[order].astype(jnp.int32)


def draw_templates(key, part):
    return template_stack(key)


def draw_owners(key, part):
    return owner_list(key)


def draw_science(key, part):
    stored = template_stack(key)[:, 0]
    chosen = stored[owner_list(key)]
    keys = jax.random.split(jax.random.fold_in(key, 37), 3)
    level = jax.random.uniform(keys[0], (3, STEPS, VISITS), jnp.float32, -0.3, 0.3)
    level = level + jnp.array([0.8, 0.0, 0.0], jnp.float32)[:, None, None]
    slope = jax.random.uniform(keys[1], (3, STEPS, VISITS), jnp.float32, -0.4, 0.4)
    position = jnp.arange(ROWS).astype(jnp.float32) / ROWS - 0.5
    factor = level[..., None] + slope[..., None] * position
    col_shift = jnp.roll(chosen, 1, axis=2)
    row_shift = jnp.roll(chosen, 2, axis=1)
    mixed = factor[0][..., None] * chosen[:, None] + factor[1][..., None] * col_shift[:, None] + factor[2][..., None] * row_shift[:, None]
    noise = 0.3 * jax.random.truncated_normal(keys[2], -4.0, 4.0, (STEPS, VISITS, ROWS, COLS), jnp.float32)
    return mixed + noise


def set_ends(result, stream_key, least, high):
    longest = result.shape.index(max(result.shape))
    spots = []
    for shift in (0, 1):
        where = [jax.random.randint(jax.random.fold_in(stream_key, axis), (), 0, length) for axis, length in enumerate(result.shape)]
        where[longest] = (where[longest] + shift) % result.shape[longest]
        spots.append(tuple(where))
    return result.at[spots[0]].set(least).at[spots[1]].set(high)


def steps_of(own_key, extent, shards, smallest, largest):
    loudness, own = 1.0, jax.random.fold_in(own_key, 6)
    for axis_at, shards_of in shards:
        heights = jnp.exp(jax.random.uniform(jax.random.fold_in(own, axis_at), (shards_of,), jnp.float32, smallest / len(shards), largest / len(shards)))
        loudness = loudness * jnp.repeat(heights, extent[axis_at] // shards_of).reshape([-1 if axis == axis_at else 1 for axis in range(len(extent))])
    return loudness


def setup_inputs(seed: int = 0) -> dict:
    streams_of = jax.random.split(jax.random.key(seed), 6)
    return {
        "templates": draw_templates(jax.random.fold_in(streams_of[5], 71), 0),
        "owners": draw_owners(jax.random.fold_in(streams_of[5], 71), 0),
        "science": draw_science(jax.random.fold_in(streams_of[5], 71), 0),
        "sci_var": jnp.clip(jnp.exp(math.log(0.3) - 2.3025852 * jax.random.uniform(streams_of[3], (STEPS, VISITS, ROWS, COLS), jnp.float32) ** steps_of(streams_of[3], (STEPS, VISITS, ROWS, COLS), ((1, 8), (2, 4)), -0.2, 0.2)), 0.03, 0.3),
        "bad_pixels": set_ends((jax.random.randint(streams_of[4], (STEPS, VISITS, ROWS, COLS), 0, 16) < 1).astype(jnp.int32), jax.random.fold_in(streams_of[4], 1), 0, 1),
    }


ridge = 1.0

def profile_table():
    offsets = np.arange(-RAD, RAD + 1) * 1.0
    recipe = [(1.0, 0), (1.5, 1), (2.0, 2), (3.0, 0), (4.0, 1)]
    profiles = []
    for spread, degree in recipe[:NPROF]:
        profile = offsets ** degree * np.exp(-offsets * offsets / (2.0 * spread * spread))
        for earlier in profiles:
            profile = profile - np.dot(earlier, profile) * earlier
        profile = profile / np.sqrt(np.dot(profile, profile))
        profiles.append(profile)
    return np.stack(profiles)

def basis_images(extended):
    profiles = jnp.asarray(profile_table(), jnp.float32)
    height = extended.shape[0] - 2 * RAD
    across = extended.shape[1]
    widened = jnp.pad(extended, ((0, 0), (RAD, RAD)))
    columns = jnp.zeros((NPROF, extended.shape[0], across), jnp.float32)
    for offset in range(2 * RAD + 1):
        columns = columns + profiles[:, offset, None, None] * widened[None, :, offset:offset + across]
    images = jnp.zeros((NPROF, NPROF, height, across), jnp.float32)
    for offset in range(2 * RAD + 1):
        images = images + profiles[None, :, offset, None, None] * columns[:, None, offset:offset + height, :]
    return images.reshape(NPROF * NPROF, height, across)

def solve_kernel(normal_mat, normal_rhs):
    count = normal_mat.shape[0]
    factor = jnp.linalg.cholesky(normal_mat + ridge * jnp.eye(count, dtype=jnp.float32))
    return jax.scipy.linalg.cho_solve((factor, True), normal_rhs)

def reference(templates, owners, science, sci_var, bad_pixels):
    results = []
    for current in range(STEPS):
        arrived = templates[owners[current]]
        extended = jnp.pad(arrived[0], ((RAD, RAD), (0, 0)))
        images = basis_images(extended)
        flattened = images.reshape(NPROF * NPROF, -1)
        tile_var = arrived[1]

        def fit_visit(pieces):
            image_sci, var_sci, bad_one = pieces
            usable = (1 - bad_one).astype(jnp.float32)
            noise_var = var_sci + tile_var
            weight = usable / noise_var
            normal_mat = jnp.dot((images * weight[None]).reshape(NPROF * NPROF, -1), flattened.T, precision=lax.Precision.HIGHEST)
            normal_rhs = jnp.dot(flattened, (weight * image_sci).reshape(-1), precision=lax.Precision.HIGHEST)
            kernel_coef = solve_kernel(normal_mat, normal_rhs)
            fitted = jnp.dot(kernel_coef, flattened, precision=lax.Precision.HIGHEST).reshape(image_sci.shape)
            return usable * (image_sci - fitted) / jnp.sqrt(noise_var)
        results.append(lax.map(fit_visit, (science[current], sci_var[current], bad_pixels[current])))
    return jnp.stack(results)
```

```python
import jax
import jax.numpy as jnp
import numpy as np
from jax import lax
from jax.experimental import pallas as pl
from jax.experimental.pallas import tpu as pltpu
from jax.sharding import PartitionSpec as P

NPROF = 5
RAD = 10
STEPS = 2
SUB = 8
LANE = 128

GROUPS = NPROF - 1
STACK = GROUPS * SUB
SPARE = SUB - NPROF
SCI_ROW = 2 * SUB + NPROF
SPOTS = [i * SUB + j for i in range(GROUPS) for j in range(NPROF)]
SPOTS += [(j // SPARE) * SUB + NPROF + j % SPARE for j in range(NPROF)]

PIVOTS = 9

PIECES = 2

FIRST_CHUNK, SECOND_CHUNK = 2 * LANE, 4 * LANE

ridge = 1.0


def profile_table():
    offsets = np.arange(-RAD, RAD + 1) * 1.0
    recipe = [(1.0, 0), (1.5, 1), (2.0, 2), (3.0, 0), (4.0, 1)]
    profiles = []
    for spread, degree in recipe[:NPROF]:
        profile = offsets**degree * np.exp(-offsets * offsets / (2.0 * spread * spread))
        for earlier in profiles:
            profile = profile - np.dot(earlier, profile) * earlier
        profile = profile / np.sqrt(np.dot(profile, profile))
        profiles.append(profile)
    return np.stack(profiles)


PARITY = [0, 1, 0, 0, 1]


def split_bf16(x, parts):
    pieces = []
    for _ in range(parts - 1):
        piece = x.astype(jnp.bfloat16).astype(jnp.float32)
        pieces.append(piece)
        x = x - piece
    return pieces + [x]


EXTRA = RAD % SUB
SLOTS = SUB // EXTRA


def vertical_table(rows):
    profiles = profile_table()
    near = RAD - EXTRA
    blank = [None] * (SUB - EXTRA)
    own = list(range(rows))
    above = [list(range(-near, 0)), list(range(-RAD, -near)) + blank]
    below = [list(range(rows, rows + near)), list(range(rows + near, rows + RAD)) + blank]
    both = []
    for inside, across, shift in ((below, above, RAD), (above, below, 0)):
        order = [(k + shift) % rows for k in range(rows)]
        joined = []
        for outputs, blocks in ((order, [own] + inside), (order[rows - RAD :], across)):
            tables = []
            for block in blocks:
                table = np.zeros((len(outputs) * SUB, len(block)), np.float32)
                for n, r in enumerate(outputs):
                    for j in range(NPROF):
                        for e, offset in enumerate(block):
                            if offset is not None and abs(offset - r) <= RAD:
                                table[n * SUB + j, e] = profiles[j, offset - r + RAD]
                hi = table.astype(jnp.bfloat16).astype(np.float32)
                mid = (table - hi).astype(jnp.bfloat16).astype(np.float32)
                low = table - hi - mid
                tables += [hi, hi, mid, hi, mid, low]
            joined.append(np.concatenate(tables, axis=1))
        width = max(table.shape[1] for table in joined)
        joined = [np.pad(table, ((0, 0), (0, width - table.shape[1]))) for table in joined]
        both.append(np.concatenate(joined, axis=0))
    return jnp.asarray(np.stack(both), jnp.bfloat16)


def patch_parity():
    return lax.rem(lax.axis_index("patch"), 2)


def six_products(hi, mid, low):
    return [hi, mid, hi, low, mid, hi]


def vmem_specs(count):
    return [pl.BlockSpec(memory_space=pltpu.VMEM)] * count


def grant(mebibytes):
    return pltpu.CompilerParams(vmem_limit_bytes=mebibytes * 1024 * 1024)


def estimate(operations):
    return pl.CostEstimate(flops=operations, bytes_accessed=1024 * 1024, transcendentals=0)


def pick_kernel(visits, per, owners, science, table, got, out):
    turn = (visits // 2) * patch_parity()
    for s in range(STEPS):
        place = lax.rem(owners[s] + turn, jnp.full((SUB, LANE), visits))
        for n in range(per):
            chosen = got[n]
            for v in range(1, visits):
                chosen = jnp.where(place == v, got[v * per + n], chosen)
            for v in range(visits):
                out[v, s, n] = chosen


def exchange(blocks):
    visits, patches = lax.axis_size("visit"), lax.axis_size("patch")
    groups = [
        [(n + (visits // 2) * (p % 2)) % visits * patches + p for n in range(visits)]
        for p in range(patches)
    ]
    return lax.all_to_all(
        blocks, ("visit", "patch"), 0, 0, axis_index_groups=groups, tiled=True
    )


def choose_owned(own, owners, science, table):
    visits = lax.axis_size("visit")
    shape = own.shape
    rows, cols = shape[-2:]
    tiles = own.reshape(shape[0], rows // SUB, SUB, cols // LANE, LANE)
    tiles = jnp.transpose(tiles, (0, 1, 3, 2, 4)).reshape(-1, SUB, LANE)
    per = tiles.shape[0] // visits
    got = exchange(tiles)

    def pick(*refs):
        pick_kernel(visits, per, *refs)

    return pl.pallas_call(
        pick,
        out_shape=jax.ShapeDtypeStruct((visits, STEPS, per, SUB, LANE), jnp.float32),
        in_specs=vmem_specs(1) + [pl.BlockSpec(memory_space=pl.ANY)] * 2 + vmem_specs(1),
        out_specs=vmem_specs(1)[0],
        compiler_params=grant(8),
    )(owners, science, table, got)


def stage_kernel(owners_in, table_in, owners, table):
    owners[...] = owners_in[...]
    table[...] = table_in[...]


def row_cells(ref, s, image, row_tile, shape):
    rows, cols, per = shape
    start = (image * (rows // SUB) + row_tile) * (cols // LANE)
    found = [ref[t // per, s, t % per] for t in range(start, start + cols // LANE)]
    return jnp.concatenate(found, axis=1)


def columns_in_parts(piece):
    profiles = profile_table()
    cols = piece.shape[1]
    width = cols + LANE
    wide = jnp.concatenate([piece, jnp.zeros((SUB, LANE), jnp.float32)], axis=1)
    totals = [piece * float(profiles[i, RAD]) if PARITY[i] == 0 else None for i in range(NPROF)]
    for d in range(1, RAD + 1):
        ahead = pltpu.roll(wide, width - d, 1)[:, :cols]
        behind = pltpu.roll(wide, d, 1)[:, :cols]
        both = (ahead + behind, ahead - behind)
        for i in range(NPROF):
            term = both[PARITY[i]] * float(profiles[i, RAD + d])
            totals[i] = term if totals[i] is None else totals[i] + term
        yield
    return totals


def advance(parts, count=None):
    while count is None or count > 0:
        try:
            next(parts)
        except StopIteration as stop:
            return stop.value
        count = None if count is None else count - 1
    return None


def along_columns(piece):
    return advance(columns_in_parts(piece))


def pass_own_rows(shape, parity, arrived, science_in, signed_var, columns, weights, scale, science):
    rows, cols, _ = shape
    row_tiles = rows // SUB
    sub = lax.broadcasted_iota(jnp.int32, (SUB, cols), 0)

    def put(ref, s, tiles):
        if parity == 0:
            moved = [pltpu.roll(tile, SUB - RAD % SUB, 0) for tile in tiles]
            tiles = []
            for t in range(row_tiles):
                near = (t + RAD // SUB) % row_tiles
                far = (near + 1) % row_tiles
                tiles.append(jnp.where(sub < SUB - RAD % SUB, moved[near], moved[far]))
        for t, tile in enumerate(tiles):
            ref[s, t * SUB : (t + 1) * SUB, :] = tile

    for s in range(STEPS):
        found = [along_columns(row_cells(arrived, s, 0, t, shape)) for t in range(row_tiles)]
        for i in range(NPROF):
            column = jnp.concatenate([piece[i] for piece in found], axis=0)
            for n, piece in enumerate(split_bf16(column, 3)):
                columns[s, i, n] = piece.astype(jnp.bfloat16)
        found = []
        for t in range(row_tiles):
            here = slice(t * SUB, (t + 1) * SUB)
            sci_var = signed_var[s, 0, here, :]
            usable = jnp.where(sci_var > 0.0, 1.0, 0.0)
            noise_var = jnp.abs(sci_var) + row_cells(arrived, s, 1, t, shape)
            found.append(usable / noise_var)
            scale[s, here, :] = usable * lax.rsqrt(noise_var)
        put(weights, s, found)
        put(science, s, [science_in[s, 0, t * SUB : (t + 1) * SUB, :] for t in range(row_tiles)])


def pack_kernel(shape, arrived, science, signed_var, across, inside, *own):
    rows, cols, _ = shape
    last = rows // SUB - 1
    col_tiles = cols // LANE
    odd = jnp.full((SUB, LANE), patch_parity()) == 1
    slot = lax.broadcasted_iota(jnp.int32, (SUB, LANE), 0) // EXTRA
    for s in range(STEPS):
        cells = [row_cells(arrived, s, 0, t, shape) for t in (0, 1, last - 1, last)]
        for group in range(col_tiles // SLOTS):
            tail, head = None, None
            for q in range(SLOTS):
                c = group * SLOTS + q
                there = slice(c * LANE, (c + 1) * LANE)
                first, second, before, final = (cell[:, there] for cell in cells)
                across[s, c] = jnp.where(odd, final, first)
                inside[s, c] = jnp.where(odd, first, final)
                low = pltpu.roll(before, (q + 1) * EXTRA, 0)
                high = pltpu.roll(second, q * EXTRA, 0)
                tail = low if tail is None else jnp.where(slot == q, low, tail)
                head = high if head is None else jnp.where(slot == q, high, head)
            across[s, col_tiles + group] = jnp.where(odd, tail, head)
            inside[s, col_tiles + group] = jnp.where(odd, head, tail)

    @pl.when(patch_parity() == 1)
    def _():
        pass_own_rows(shape, 1, arrived, science, signed_var, *own)


def own_kernel(shape, arrived, science, signed_var, *refs):
    @pl.when(patch_parity() == 0)
    def _():
        pass_own_rows(shape, 0, arrived, science, signed_var, *refs[len(refs) // 2 :])


def near_columns(halo, s, cols):
    return columns_in_parts(jnp.concatenate([halo[s, c] for c in range(cols // LANE)], axis=1))


def extra_columns(halo, cols):
    sub = lax.broadcasted_iota(jnp.int32, (SUB, LANE), 0)
    col_tiles = cols // LANE
    extra = []
    for c in range(col_tiles):
        found = None
        for s in range(STEPS):
            moved = pltpu.roll(
                halo[s, col_tiles + c // SLOTS], (SUB + (s - c % SLOTS) * EXTRA) % SUB, 0
            )
            found = moved if found is None else jnp.where(sub < s * EXTRA, found, moved)
        extra.append(found)
    extra = along_columns(jnp.concatenate(extra, axis=1))
    return [[pltpu.roll(x, SUB - s * EXTRA, 0) if s else x for x in extra] for s in range(STEPS)]


def split_tile(tile):
    return jnp.concatenate(six_products(*split_bf16(tile, 3)), axis=0).astype(jnp.bfloat16)


def fit_rows(s, first, count, there, images, weights, science, stack):
    sub = lax.broadcasted_iota(jnp.int32, (SUB, there.stop - there.start), 0)
    total = None
    for n in range(count):
        k = first + n
        here = slice(n * SUB, (n + 1) * SUB)
        last = images[GROUPS][here, :]
        groups = []
        for i in range(GROUPS):
            found = images[i][here, :]
            if i < 2:
                turn = (NPROF - i * SPARE) % SUB
                found = jnp.where(sub < NPROF, found, pltpu.roll(last, turn, 0))
            elif i == 2:
                found = jnp.where(sub == NPROF, science[s, k : k + 1, there], found)
            stack[s, n, i * SUB : (i + 1) * SUB, there] = found
            groups.append(found)
        found = jnp.concatenate(groups, axis=0)
        hi = found.astype(jnp.bfloat16)
        mid = (found - hi.astype(jnp.float32)).astype(jnp.bfloat16)
        rounded = (found * weights[s, k : k + 1, there]).astype(jnp.bfloat16)
        product = lax.dot_general(
            jnp.concatenate([rounded, rounded], axis=1),
            jnp.concatenate([hi, mid], axis=1),
            (((1,), (1,)), ((), ())),
            preferred_element_type=jnp.float32,
        )
        total = product if total is None else total + product
    return total


def fit_chunks(halo, cols, chunk, first, count, vertical, weights, science, stack):
    extra = extra_columns(halo, cols)
    near = advance(near_columns(halo, 0, cols))
    starts = range(0, cols, chunk)
    items = [(s, slice(start, start + chunk)) for s in range(STEPS) for start in starts]
    images = vertical(0, items[0][1], near, extra[0])
    totals = [None] * STEPS
    coming = None
    for n, (s, there) in enumerate(items):
        following = items[n + 1] if n + 1 < len(items) else None
        if following is not None:
            if s + 1 < STEPS:
                if coming is None:
                    coming, found = near_columns(halo, s + 1, cols), None
                share = None if following[0] != s else -(-RAD // (len(starts) - 1))
                found = advance(coming, share) if found is None else found
            if following[0] != s:
                near, coming = found, None
            upcoming = vertical(*following, near, extra[following[0]])
        total = fit_rows(s, first, count, there, images, weights, science, stack)
        totals[s] = total if totals[s] is None else totals[s] + total
        images = upcoming if following is not None else None
    sides = []
    for total in totals:
        sides.append(total)
        sides.append(jnp.zeros((STACK, LANE // STEPS - STACK), jnp.float32))
    return jnp.concatenate(sides, axis=1)


def first_kernel(shape, inside, own, weights, science, table, normal, stack, partial):
    rows, cols, _ = shape
    early = rows - RAD

    def vertical(s, there, near, extra):
        images = []
        for i in range(NPROF):
            spread = six_products(*(own[s, i, n, :, there] for n in range(3)))
            spread += [split_tile(near[i][:, there]), split_tile(extra[i][:, there])]
            image = jnp.dot(
                table[patch_parity(), : rows * SUB, :],
                jnp.concatenate(spread, axis=0),
                preferred_element_type=jnp.float32,
            )
            images.append(image[: early * SUB, :])
            partial[s, i, :, there] = image[early * SUB :, :]
        return images

    normal[...] = fit_chunks(inside, cols, FIRST_CHUNK, 0, early, vertical, weights, science, stack)


def second_kernel(shape, across, weights, science, table, before, partial, normal, stack):
    rows, cols, _ = shape

    def vertical(s, there, near, extra):
        images = []
        for i in range(NPROF):
            spread = [split_tile(near[i][:, there]), split_tile(extra[i][:, there])]
            spread = jnp.concatenate(spread, axis=0)
            image = jnp.dot(
                table[patch_parity(), rows * SUB :, : spread.shape[0]],
                spread,
                preferred_element_type=jnp.float32,
            )
            images.append(partial[s, i, :, there] + image)
        return images

    found = fit_chunks(
        across, cols, SECOND_CHUNK, rows - RAD, RAD, vertical, weights, science, stack
    )
    normal[...] = before[...] + found


def solve_both(blocks):
    half = LANE // STEPS
    sub = lax.broadcasted_iota(jnp.int32, (SUB, LANE), 0)
    lane = lax.broadcasted_iota(jnp.int32, (SUB, LANE), 1)

    def spread(k):
        return [
            jnp.where(lane < half, block[:, k : k + 1], block[:, half + k : half + k + 1])
            for block in blocks
        ]

    def entry(column, k):
        row = column[k // SUB][k % SUB : k % SUB + 1, :]
        return jnp.broadcast_to(row, (SUB, LANE))

    for start in range(0, len(SPOTS), PIVOTS):
        spots = SPOTS[start : start + PIVOTS]
        columns = [spread(k) for k in spots]
        inner = [[entry(column, k) for column in columns] for k in spots]
        rows = [entry(blocks, k) for k in spots]
        for t in range(len(spots)):
            inverse = 1.0 / inner[t][t]
            inner[t] = [x * inverse for x in inner[t]]
            rows[t] = rows[t] * inverse
            for n in range(len(spots)):
                if n != t:
                    factor = inner[n][t]
                    inner[n] = [x - factor * y for x, y in zip(inner[n], inner[t])]
                    rows[n] = rows[n] - factor * rows[t]
        updated = []
        for i, block in enumerate(blocks):
            terms = [column[i] * row for column, row in zip(columns, rows)]
            while len(terms) > 1:
                terms = [sum(terms[n : n + 2][1:], terms[n]) for n in range(0, len(terms), 2)]
            block = block - terms[0]
            for k, row in zip(spots, rows):
                if k // SUB == i:
                    block = jnp.where(sub == k % SUB, row, block)
            updated.append(block)
        blocks = updated
    return blocks


def fold_rows(found):
    sub = lax.broadcasted_iota(jnp.int32, found[0].shape, 0)
    hop = SUB // 2
    while hop:
        upper = (sub & hop) != 0
        count = len(found) // 2
        joined = []
        for low, high in zip(found[:count], found[count:]):
            kept = jnp.where(upper, high, low)
            if 2 * hop == SUB:
                moved = pltpu.roll(jnp.where(upper, low, high), hop, 0)
            else:
                moved = jnp.where(
                    upper, pltpu.roll(high, hop, 0), pltpu.roll(low, SUB - hop, 0)
                )
            joined.append(kept + moved)
        found = joined
        hop //= 2
    return found[0]


def solve_kernel(rows, cols, count, *refs):
    parts, (scale, early, late, out, held, sems) = refs[:count], refs[count:]
    copies = []
    odd = jnp.full((SUB, LANE), patch_parity()) == 1
    turn = rows - RAD
    half = LANE // STEPS
    sub = lax.broadcasted_iota(jnp.int32, (SUB, LANE), 0)
    lane = lax.broadcasted_iota(jnp.int32, (SUB, LANE), 1)
    blocks = []
    for start in range(0, STACK, SUB):
        block = jnp.where(lax.rem(lane, half) == sub + start, ridge, 0.0)
        for part in parts:
            block = block + part[start : start + SUB, :]
        blocks.append(block)
    solved = solve_both(blocks)
    for s in range(STEPS):
        factors = []
        for i in range(GROUPS):
            spot = s * half + SCI_ROW
            factor = jnp.broadcast_to(solved[i][:, spot : spot + 1], (SUB, LANE))
            used = [k % SUB for k in SPOTS if k // SUB == i]
            if len(used) < SUB:
                factor = jnp.where(sub < len(used), factor, 0.0)
            if i == SCI_ROW // SUB:
                factor = jnp.where(sub == SCI_ROW % SUB, -1.0, factor)
            factors.append(factor)
        for c in range(cols // LANE):
            there = slice(c * LANE, (c + 1) * LANE)
            found = []
            for k in range(rows):
                source, n = (early, k) if k < turn else (late, k - turn)
                total = source[s, n, 0:SUB, there] * factors[0]
                for i in range(1, GROUPS):
                    total = total + source[s, n, i * SUB : (i + 1) * SUB, there] * factors[i]
                found.append(total)
            tiles = [fold_rows(found[k : k + SUB]) for k in range(0, rows, SUB)]
            moved = [pltpu.roll(tile, (SUB - turn) % SUB, 0) for tile in tiles]
            for t, tile in enumerate(tiles):
                after = (t + turn // SUB) % len(tiles)
                ahead = (after + 1) % len(tiles)
                turned = jnp.where(sub < SUB - turn % SUB, moved[after], moved[ahead])
                here = slice(t * SUB, (t + 1) * SUB)
                left = jnp.where(odd, tile, turned)
                held[s, 0, here, there] = -left * scale[s, here, there]
            if there.stop % (cols // PIECES) == 0:
                whole = (s, slice(None), slice(None), pl.ds(there.stop - cols // PIECES, cols // PIECES))
                copy = pltpu.make_async_copy(held.at[whole], out.at[whole], sems.at[len(copies)])
                copy.start()
                copies.append(copy)
    for copy in copies:
        copy.wait()


def shards(templates, owners, science, sci_var, bad_pixels):
    rows, cols = templates.shape[-2:]
    image = jax.ShapeDtypeStruct((STEPS, rows, cols), jnp.float32)
    held = jax.ShapeDtypeStruct(science.shape, jnp.float32)
    bad = bad_pixels != 0
    science = jnp.where(bad, 0.0, science)
    signed_var = jnp.where(bad, -sci_var, sci_var)
    table = vertical_table(rows)
    owners = jnp.broadcast_to(owners[:, None, None], (STEPS, SUB, LANE))
    owners, table = pl.pallas_call(
        stage_kernel,
        out_shape=[jax.ShapeDtypeStruct(x.shape, x.dtype) for x in (owners, table)],
        in_specs=vmem_specs(2),
        out_specs=vmem_specs(2),
        compiler_params=grant(8),
        cost_estimate=estimate(1 << 20),
    )(owners, table)
    chosen = choose_owned(templates[0], owners, science, table)
    arrived = exchange(chosen)
    visits, per = arrived.shape[0], arrived.shape[2]
    shape = (rows, cols, per)

    own_shapes = (
        jax.ShapeDtypeStruct((STEPS, NPROF, 3, rows, cols), jnp.bfloat16),
        image,
        image,
        image,
    )

    def pack(*refs):
        pack_kernel(shape, *refs)

    tiles = cols // LANE
    packed = jax.ShapeDtypeStruct((STEPS, tiles + tiles // SLOTS, SUB, LANE), jnp.float32)
    across, inside, *own = pl.pallas_call(
        pack,
        out_shape=(packed, packed) + own_shapes,
        in_specs=vmem_specs(3),
        out_specs=vmem_specs(6),
        compiler_params=grant(8),
    )(arrived, science, signed_var)
    patches = lax.axis_size("patch")
    swaps = [(i, i + 1) for i in range(1, patches - 1, 2)]
    across = lax.ppermute(across, "patch", swaps + [(b, a) for a, b in swaps])
    inside = lax.ppermute(inside, "patch", [(i, i ^ 1) for i in range(patches)])

    def own_rows(*refs):
        own_kernel(shape, *refs)

    columns, weights, scale, science = pl.pallas_call(
        own_rows,
        out_shape=own_shapes,
        in_specs=vmem_specs(7),
        out_specs=vmem_specs(4),
        input_output_aliases={3: 0, 4: 1, 5: 2, 6: 3},
        compiler_params=grant(8),
        cost_estimate=estimate(1 << 28),
    )(arrived, science, signed_var, *own)

    def first(*refs):
        first_kernel(shape, *refs)

    def second(*refs):
        second_kernel(shape, *refs)

    normal = jax.ShapeDtypeStruct((STACK, LANE), jnp.float32)
    part, early_images, partial = pl.pallas_call(
        first,
        out_shape=(
            normal,
            jax.ShapeDtypeStruct((STEPS, rows - RAD, STACK, cols), jnp.float32),
            jax.ShapeDtypeStruct((STEPS, NPROF, RAD * SUB, cols), jnp.float32),
        ),
        in_specs=vmem_specs(5),
        out_specs=vmem_specs(3),
        compiler_params=grant(16),
        cost_estimate=estimate(1 << 28),
    )(inside, columns, weights, science, table)
    part, late_images = pl.pallas_call(
        second,
        out_shape=(normal, jax.ShapeDtypeStruct((STEPS, RAD, STACK, cols), jnp.float32)),
        in_specs=vmem_specs(6),
        out_specs=vmem_specs(2),
        compiler_params=grant(16),
        cost_estimate=estimate(1 << 28),
    )(across, weights, science, table, part, partial)

    parts, group = [part], 1
    while group < patches:
        if group > 1:
            parts = [sum(parts[1:], parts[0])]
        size = min(4, patches // group)
        for hop in range(group, size * group, group):
            pairs = [(i, i ^ hop) for i in range(patches)]
            parts.append(lax.ppermute(parts[0], "patch", pairs))
        group *= size

    def solve(*refs):
        solve_kernel(rows, cols, len(parts), *refs)

    return pl.pallas_call(
        solve,
        out_shape=held,
        in_specs=vmem_specs(len(parts) + 3),
        out_specs=pl.BlockSpec(memory_space=pl.ANY),
        scratch_shapes=[
            pltpu.VMEM(held.shape, held.dtype),
            pltpu.SemaphoreType.DMA((STEPS * PIECES,)),
        ],
        compiler_params=grant(16),
    )(*parts, scale, early_images, late_images)


def solution(mesh):
    return jax.shard_map(
        shards,
        mesh=mesh,
        in_specs=(
            P("visit", None, "patch", None),
            P(),
            P(None, "visit", "patch", None),
            P(None, "visit", "patch", None),
            P(None, "visit", "patch", None),
        ),
        out_specs=P(None, "visit", "patch", None),
        check_vma=False,
    )
```

```python
import jax
import jax.numpy as jnp
import numpy as np
from jax import lax
from jax.experimental import pallas as pl
from jax.experimental.pallas import tpu as pltpu
from jax.sharding import PartitionSpec as P

NPROF = 5
RAD = 10
STEPS = 2
SUB = 8
LANE = 128

GROUPS = NPROF - 1
STACK = GROUPS * SUB
SPARE = SUB - NPROF
SCI_ROW = 2 * SUB + NPROF
SPOTS = [i * SUB + j for i in range(GROUPS) for j in range(NPROF)]
SPOTS += [(j // SPARE) * SUB + NPROF + j % SPARE for j in range(NPROF)]

PIVOTS = 9

PIECES = 2

FIRST_CHUNK, SECOND_CHUNK = 2 * LANE, 4 * LANE

ridge = 1.0


def profile_table():
    offsets = np.arange(-RAD, RAD + 1) * 1.0
    recipe = [(1.0, 0), (1.5, 1), (2.0, 2), (3.0, 0), (4.0, 1)]
    profiles = []
    for spread, degree in recipe[:NPROF]:
        profile = offsets**degree * np.exp(-offsets * offsets / (2.0 * spread * spread))
        for earlier in profiles:
            profile = profile - np.dot(earlier, profile) * earlier
        profile = profile / np.sqrt(np.dot(profile, profile))
        profiles.append(profile)
    return np.stack(profiles)


PARITY = [0, 1, 0, 0, 1]


def split_bf16(x, parts):
    pieces = []
    for _ in range(parts - 1):
        piece = x.astype(jnp.bfloat16).astype(jnp.float32)
        pieces.append(piece)
        x = x - piece
    return pieces + [x]


EXTRA = RAD % SUB
SLOTS = SUB // EXTRA


def vertical_table(rows):
    profiles = profile_table()
    near = RAD - EXTRA
    blank = [None] * (SUB - EXTRA)
    own = list(range(rows))
    above = [list(range(-near, 0)), list(range(-RAD, -near)) + blank]
    below = [list(range(rows, rows + near)), list(range(rows + near, rows + RAD)) + blank]
    both = []
    for inside, across, shift in ((below, above, RAD), (above, below, 0)):
        order = [(k + shift) % rows for k in range(rows)]
        joined = []
        for outputs, blocks in ((order, [own] + inside), (order[rows - RAD :], across)):
            tables = []
            for block in blocks:
                table = np.zeros((len(outputs) * SUB, len(block)), np.float32)
                for n, r in enumerate(outputs):
                    for j in range(NPROF):
                        for e, offset in enumerate(block):
                            if offset is not None and abs(offset - r) <= RAD:
                                table[n * SUB + j, e] = profiles[j, offset - r + RAD]
                hi = table.astype(jnp.bfloat16).astype(np.float32)
                mid = (table - hi).astype(jnp.bfloat16).astype(np.float32)
                low = table - hi - mid
                tables += [hi, hi, mid, hi, mid, low]
            joined.append(np.concatenate(tables, axis=1))
        width = max(table.shape[1] for table in joined)
        joined = [np.pad(table, ((0, 0), (0, width - table.shape[1]))) for table in joined]
        both.append(np.concatenate(joined, axis=0))
    return jnp.asarray(np.stack(both), jnp.bfloat16)


def patch_parity():
    return lax.rem(lax.axis_index("patch"), 2)


def six_products(hi, mid, low):
    return [hi, mid, hi, low, mid, hi]


def vmem_specs(count):
    return [pl.BlockSpec(memory_space=pltpu.VMEM)] * count


def grant(mebibytes):
    return pltpu.CompilerParams(vmem_limit_bytes=mebibytes * 1024 * 1024)


def estimate(operations):
    return pl.CostEstimate(flops=operations, bytes_accessed=1024 * 1024, transcendentals=0)


def pick_kernel(visits, per, owners, science, table, got, out):
    turn = visits - visits // 2 - 1 + patch_parity()
    for s in range(STEPS):
        place = lax.rem(owners[s] + turn, jnp.full((SUB, LANE), visits))
        for n in range(per):
            chosen = got[n]
            for v in range(1, visits):
                chosen = jnp.where(place == v, got[v * per + n], chosen)
            for v in range(visits):
                out[v, s, n] = chosen


def exchange(blocks):
    visits, patches = lax.axis_size("visit"), lax.axis_size("patch")
    groups = [
        [(n + visits // 2 + 1 - p % 2) % visits * patches + p for n in range(visits)]
        for p in range(patches)
    ]
    return lax.all_to_all(
        blocks, ("visit", "patch"), 0, 0, axis_index_groups=groups, tiled=True
    )


def choose_owned(own, owners, science, table):
    visits = lax.axis_size("visit")
    shape = own.shape
    rows, cols = shape[-2:]
    tiles = own.reshape(shape[0], rows // SUB, SUB, cols // LANE, LANE)
    tiles = jnp.transpose(tiles, (0, 1, 3, 2, 4)).reshape(-1, SUB, LANE)
    per = tiles.shape[0] // visits
    got = exchange(tiles)

    def pick(*refs):
        pick_kernel(visits, per, *refs)

    return pl.pallas_call(
        pick,
        out_shape=jax.ShapeDtypeStruct((visits, STEPS, per, SUB, LANE), jnp.float32),
        in_specs=vmem_specs(1) + [pl.BlockSpec(memory_space=pl.ANY)] * 2 + vmem_specs(1),
        out_specs=vmem_specs(1)[0],
        compiler_params=grant(8),
    )(owners, science, table, got)


def stage_kernel(owners_in, table_in, owners, table):
    owners[...] = owners_in[...]
    table[...] = table_in[...]


def row_cells(ref, s, image, row_tile, shape):
    rows, cols, per = shape
    start = (image * (rows // SUB) + row_tile) * (cols // LANE)
    found = [ref[t // per, s, t % per] for t in range(start, start + cols // LANE)]
    return jnp.concatenate(found, axis=1)


def columns_in_parts(piece):
    profiles = profile_table()
    cols = piece.shape[1]
    width = cols + LANE
    wide = jnp.concatenate([piece, jnp.zeros((SUB, LANE), jnp.float32)], axis=1)
    totals = [piece * float(profiles[i, RAD]) if PARITY[i] == 0 else None for i in range(NPROF)]
    for d in range(1, RAD + 1):
        ahead = pltpu.roll(wide, width - d, 1)[:, :cols]
        behind = pltpu.roll(wide, d, 1)[:, :cols]
        both = (ahead + behind, ahead - behind)
        for i in range(NPROF):
            term = both[PARITY[i]] * float(profiles[i, RAD + d])
            totals[i] = term if totals[i] is None else totals[i] + term
        yield
    return totals


def advance(parts, count=None):
    while count is None or count > 0:
        try:
            next(parts)
        except StopIteration as stop:
            return stop.value
        count = None if count is None else count - 1
    return None


def along_columns(piece):
    return advance(columns_in_parts(piece))


def pass_own_rows(shape, parity, arrived, science_in, signed_var, columns, weights, scale, science):
    rows, cols, _ = shape
    row_tiles = rows // SUB
    sub = lax.broadcasted_iota(jnp.int32, (SUB, cols), 0)

    def put(ref, s, tiles):
        if parity == 0:
            moved = [pltpu.roll(tile, SUB - RAD % SUB, 0) for tile in tiles]
            tiles = []
            for t in range(row_tiles):
                near = (t + RAD // SUB) % row_tiles
                far = (near + 1) % row_tiles
                tiles.append(jnp.where(sub < SUB - RAD % SUB, moved[near], moved[far]))
        for t, tile in enumerate(tiles):
            ref[s, t * SUB : (t + 1) * SUB, :] = tile

    for s in range(STEPS):
        found = [along_columns(row_cells(arrived, s, 0, t, shape)) for t in range(row_tiles)]
        for i in range(NPROF):
            column = jnp.concatenate([piece[i] for piece in found], axis=0)
            for n, piece in enumerate(split_bf16(column, 3)):
                columns[s, i, n] = piece.astype(jnp.bfloat16)
        found = []
        for t in range(row_tiles):
            here = slice(t * SUB, (t + 1) * SUB)
            sci_var = signed_var[s, 0, here, :]
            usable = jnp.where(sci_var > 0.0, 1.0, 0.0)
            noise_var = jnp.abs(sci_var) + row_cells(arrived, s, 1, t, shape)
            found.append(usable / noise_var)
            scale[s, here, :] = usable * lax.rsqrt(noise_var)
        put(weights, s, found)
        put(science, s, [science_in[s, 0, t * SUB : (t + 1) * SUB, :] for t in range(row_tiles)])


def pack_kernel(shape, arrived, science, signed_var, across, inside, *own):
    rows, cols, _ = shape
    last = rows // SUB - 1
    col_tiles = cols // LANE
    odd = jnp.full((SUB, LANE), patch_parity()) == 1
    slot = lax.broadcasted_iota(jnp.int32, (SUB, LANE), 0) // EXTRA
    for s in range(STEPS):
        cells = [row_cells(arrived, s, 0, t, shape) for t in (0, 1, last - 1, last)]
        for group in range(col_tiles // SLOTS):
            tail, head = None, None
            for q in range(SLOTS):
                c = group * SLOTS + q
                there = slice(c * LANE, (c + 1) * LANE)
                first, second, before, final = (cell[:, there] for cell in cells)
                across[s, c] = jnp.where(odd, final, first)
                inside[s, c] = jnp.where(odd, first, final)
                low = pltpu.roll(before, (q + 1) * EXTRA, 0)
                high = pltpu.roll(second, q * EXTRA, 0)
                tail = low if tail is None else jnp.where(slot == q, low, tail)
                head = high if head is None else jnp.where(slot == q, high, head)
            across[s, col_tiles + group] = jnp.where(odd, tail, head)
            inside[s, col_tiles + group] = jnp.where(odd, head, tail)

    @pl.when(patch_parity() == 1)
    def _():
        pass_own_rows(shape, 1, arrived, science, signed_var, *own)


def own_kernel(shape, arrived, science, signed_var, *refs):
    @pl.when(patch_parity() == 0)
    def _():
        pass_own_rows(shape, 0, arrived, science, signed_var, *refs[len(refs) // 2 :])


def near_columns(halo, s, cols):
    return columns_in_parts(jnp.concatenate([halo[s, c] for c in range(cols // LANE)], axis=1))


def extra_columns(halo, cols):
    sub = lax.broadcasted_iota(jnp.int32, (SUB, LANE), 0)
    col_tiles = cols // LANE
    extra = []
    for c in range(col_tiles):
        found = None
        for s in range(STEPS):
            moved = pltpu.roll(
                halo[s, col_tiles + c // SLOTS], (SUB + (s - c % SLOTS) * EXTRA) % SUB, 0
            )
            found = moved if found is None else jnp.where(sub < s * EXTRA, found, moved)
        extra.append(found)
    extra = along_columns(jnp.concatenate(extra, axis=1))
    return [[pltpu.roll(x, SUB - s * EXTRA, 0) if s else x for x in extra] for s in range(STEPS)]


def split_tile(tile):
    return jnp.concatenate(six_products(*split_bf16(tile, 3)), axis=0).astype(jnp.bfloat16)


def fit_rows(s, first, count, there, images, weights, science, stack):
    sub = lax.broadcasted_iota(jnp.int32, (SUB, there.stop - there.start), 0)
    total = None
    for n in range(count):
        k = first + n
        here = slice(n * SUB, (n + 1) * SUB)
        last = images[GROUPS][here, :]
        groups = []
        for i in range(GROUPS):
            found = images[i][here, :]
            if i < 2:
                turn = (NPROF - i * SPARE) % SUB
                found = jnp.where(sub < NPROF, found, pltpu.roll(last, turn, 0))
            elif i == 2:
                found = jnp.where(sub == NPROF, science[s, k : k + 1, there], found)
            stack[s, n, i * SUB : (i + 1) * SUB, there] = found
            groups.append(found)
        found = jnp.concatenate(groups, axis=0)
        hi = found.astype(jnp.bfloat16)
        mid = (found - hi.astype(jnp.float32)).astype(jnp.bfloat16)
        rounded = (found * weights[s, k : k + 1, there]).astype(jnp.bfloat16)
        product = lax.dot_general(
            jnp.concatenate([rounded, rounded], axis=1),
            jnp.concatenate([hi, mid], axis=1),
            (((1,), (1,)), ((), ())),
            preferred_element_type=jnp.float32,
        )
        total = product if total is None else total + product
    return total


def fit_chunks(halo, cols, chunk, first, count, vertical, weights, science, stack):
    extra = extra_columns(halo, cols)
    near = advance(near_columns(halo, 0, cols))
    starts = range(0, cols, chunk)
    items = [(s, slice(start, start + chunk)) for s in range(STEPS) for start in starts]
    images = vertical(0, items[0][1], near, extra[0])
    totals = [None] * STEPS
    coming = None
    for n, (s, there) in enumerate(items):
        following = items[n + 1] if n + 1 < len(items) else None
        if following is not None:
            if s + 1 < STEPS:
                if coming is None:
                    coming, found = near_columns(halo, s + 1, cols), None
                share = None if following[0] != s else -(-RAD // (len(starts) - 1))
                found = advance(coming, share) if found is None else found
            if following[0] != s:
                near, coming = found, None
            upcoming = vertical(*following, near, extra[following[0]])
        total = fit_rows(s, first, count, there, images, weights, science, stack)
        totals[s] = total if totals[s] is None else totals[s] + total
        images = upcoming if following is not None else None
    sides = []
    for total in totals:
        sides.append(total)
        sides.append(jnp.zeros((STACK, LANE // STEPS - STACK), jnp.float32))
    return jnp.concatenate(sides, axis=1)


def first_kernel(shape, inside, own, weights, science, table, normal, stack, partial):
    rows, cols, _ = shape
    early = rows - RAD

    def vertical(s, there, near, extra):
        images = []
        for i in range(NPROF):
            spread = six_products(*(own[s, i, n, :, there] for n in range(3)))
            spread += [split_tile(near[i][:, there]), split_tile(extra[i][:, there])]
            image = jnp.dot(
                table[patch_parity(), : rows * SUB, :],
                jnp.concatenate(spread, axis=0),
                preferred_element_type=jnp.float32,
            )
            images.append(image[: early * SUB, :])
            partial[s, i, :, there] = image[early * SUB :, :]
        return images

    normal[...] = fit_chunks(inside, cols, FIRST_CHUNK, 0, early, vertical, weights, science, stack)


def second_kernel(shape, across, weights, science, table, before, partial, normal, stack):
    rows, cols, _ = shape

    def vertical(s, there, near, extra):
        images = []
        for i in range(NPROF):
            spread = [split_tile(near[i][:, there]), split_tile(extra[i][:, there])]
            spread = jnp.concatenate(spread, axis=0)
            image = jnp.dot(
                table[patch_parity(), rows * SUB :, : spread.shape[0]],
                spread,
                preferred_element_type=jnp.float32,
            )
            images.append(partial[s, i, :, there] + image)
        return images

    found = fit_chunks(
        across, cols, SECOND_CHUNK, rows - RAD, RAD, vertical, weights, science, stack
    )
    normal[...] = before[...] + found


def solve_both(blocks):
    half = LANE // STEPS
    sub = lax.broadcasted_iota(jnp.int32, (SUB, LANE), 0)
    lane = lax.broadcasted_iota(jnp.int32, (SUB, LANE), 1)

    def spread(k):
        return [
            jnp.where(lane < half, block[:, k : k + 1], block[:, half + k : half + k + 1])
            for block in blocks
        ]

    def entry(column, k):
        row = column[k // SUB][k % SUB : k % SUB + 1, :]
        return jnp.broadcast_to(row, (SUB, LANE))

    for start in range(0, len(SPOTS), PIVOTS):
        spots = SPOTS[start : start + PIVOTS]
        columns = [spread(k) for k in spots]
        inner = [[entry(column, k) for column in columns] for k in spots]
        rows = [entry(blocks, k) for k in spots]
        for t in range(len(spots)):
            inverse = 1.0 / inner[t][t]
            inner[t] = [x * inverse for x in inner[t]]
            rows[t] = rows[t] * inverse
            for n in range(len(spots)):
                if n != t:
                    factor = inner[n][t]
                    inner[n] = [x - factor * y for x, y in zip(inner[n], inner[t])]
                    rows[n] = rows[n] - factor * rows[t]
        updated = []
        for i, block in enumerate(blocks):
            terms = [column[i] * row for column, row in zip(columns, rows)]
            while len(terms) > 1:
                terms = [sum(terms[n : n + 2][1:], terms[n]) for n in range(0, len(terms), 2)]
            block = block - terms[0]
            for k, row in zip(spots, rows):
                if k // SUB == i:
                    block = jnp.where(sub == k % SUB, row, block)
            updated.append(block)
        blocks = updated
    return blocks


def fold_rows(found):
    sub = lax.broadcasted_iota(jnp.int32, found[0].shape, 0)
    hop = SUB // 2
    while hop:
        upper = (sub & hop) != 0
        count = len(found) // 2
        joined = []
        for low, high in zip(found[:count], found[count:]):
            kept = jnp.where(upper, high, low)
            if 2 * hop == SUB:
                moved = pltpu.roll(jnp.where(upper, low, high), hop, 0)
            else:
                moved = jnp.where(
                    upper, pltpu.roll(high, hop, 0), pltpu.roll(low, SUB - hop, 0)
                )
            joined.append(kept + moved)
        found = joined
        hop //= 2
    return found[0]


def solve_kernel(rows, cols, count, *refs):
    parts, (scale, early, late, out, held, sems) = refs[:count], refs[count:]
    copies = []
    odd = jnp.full((SUB, LANE), patch_parity()) == 1
    turn = rows - RAD
    half = LANE // STEPS
    sub = lax.broadcasted_iota(jnp.int32, (SUB, LANE), 0)
    lane = lax.broadcasted_iota(jnp.int32, (SUB, LANE), 1)
    blocks = []
    for start in range(0, STACK, SUB):
        block = jnp.where(lax.rem(lane, half) == sub + start, ridge, 0.0)
        for part in parts:
            block = block + part[start : start + SUB, :]
        blocks.append(block)
    solved = solve_both(blocks)
    for s in range(STEPS):
        factors = []
        for i in range(GROUPS):
            spot = s * half + SCI_ROW
            factor = jnp.broadcast_to(solved[i][:, spot : spot + 1], (SUB, LANE))
            used = [k % SUB for k in SPOTS if k // SUB == i]
            if len(used) < SUB:
                factor = jnp.where(sub < len(used), factor, 0.0)
            if i == SCI_ROW // SUB:
                factor = jnp.where(sub == SCI_ROW % SUB, -1.0, factor)
            factors.append(factor)
        for c in range(cols // LANE):
            there = slice(c * LANE, (c + 1) * LANE)
            found = []
            for k in range(rows):
                source, n = (early, k) if k < turn else (late, k - turn)
                total = source[s, n, 0:SUB, there] * factors[0]
                for i in range(1, GROUPS):
                    total = total + source[s, n, i * SUB : (i + 1) * SUB, there] * factors[i]
                found.append(total)
            tiles = [fold_rows(found[k : k + SUB]) for k in range(0, rows, SUB)]
            moved = [pltpu.roll(tile, (SUB - turn) % SUB, 0) for tile in tiles]
            for t, tile in enumerate(tiles):
                after = (t + turn // SUB) % len(tiles)
                ahead = (after + 1) % len(tiles)
                turned = jnp.where(sub < SUB - turn % SUB, moved[after], moved[ahead])
                here = slice(t * SUB, (t + 1) * SUB)
                left = jnp.where(odd, tile, turned)
                held[s, 0, here, there] = -left * scale[s, here, there]
            if there.stop % (cols // PIECES) == 0:
                whole = (s, slice(None), slice(None), pl.ds(there.stop - cols // PIECES, cols // PIECES))
                copy = pltpu.make_async_copy(held.at[whole], out.at[whole], sems.at[len(copies)])
                copy.start()
                copies.append(copy)
    for copy in copies:
        copy.wait()


def shards(templates, owners, science, sci_var, bad_pixels):
    rows, cols = templates.shape[-2:]
    image = jax.ShapeDtypeStruct((STEPS, rows, cols), jnp.float32)
    held = jax.ShapeDtypeStruct(science.shape, jnp.float32)
    bad = bad_pixels != 0
    science = jnp.where(bad, 0.0, science)
    signed_var = jnp.where(bad, -sci_var, sci_var)
    table = vertical_table(rows)
    owners = jnp.broadcast_to(owners[:, None, None], (STEPS, SUB, LANE))
    owners, table = pl.pallas_call(
        stage_kernel,
        out_shape=[jax.ShapeDtypeStruct(x.shape, x.dtype) for x in (owners, table)],
        in_specs=vmem_specs(2),
        out_specs=vmem_specs(2),
        compiler_params=grant(8),
        cost_estimate=estimate(1 << 20),
    )(owners, table)
    chosen = choose_owned(templates[0], owners, science, table)
    arrived = exchange(chosen)
    visits, per = arrived.shape[0], arrived.shape[2]
    shape = (rows, cols, per)

    own_shapes = (
        jax.ShapeDtypeStruct((STEPS, NPROF, 3, rows, cols), jnp.bfloat16),
        image,
        image,
        image,
    )

    def pack(*refs):
        pack_kernel(shape, *refs)

    tiles = cols // LANE
    packed = jax.ShapeDtypeStruct((STEPS, tiles + tiles // SLOTS, SUB, LANE), jnp.float32)
    across, inside, *own = pl.pallas_call(
        pack,
        out_shape=(packed, packed) + own_shapes,
        in_specs=vmem_specs(3),
        out_specs=vmem_specs(6),
        compiler_params=grant(8),
    )(arrived, science, signed_var)
    patches = lax.axis_size("patch")
    swaps = [(i, i + 1) for i in range(1, patches - 1, 2)]
    across = lax.ppermute(across, "patch", swaps + [(b, a) for a, b in swaps])
    inside = lax.ppermute(inside, "patch", [(i, i ^ 1) for i in range(patches)])

    def own_rows(*refs):
        own_kernel(shape, *refs)

    columns, weights, scale, science = pl.pallas_call(
        own_rows,
        out_shape=own_shapes,
        in_specs=vmem_specs(7),
        out_specs=vmem_specs(4),
        input_output_aliases={3: 0, 4: 1, 5: 2, 6: 3},
        compiler_params=grant(8),
        cost_estimate=estimate(1 << 28),
    )(arrived, science, signed_var, *own)

    def first(*refs):
        first_kernel(shape, *refs)

    def second(*refs):
        second_kernel(shape, *refs)

    normal = jax.ShapeDtypeStruct((STACK, LANE), jnp.float32)
    part, early_images, partial = pl.pallas_call(
        first,
        out_shape=(
            normal,
            jax.ShapeDtypeStruct((STEPS, rows - RAD, STACK, cols), jnp.float32),
            jax.ShapeDtypeStruct((STEPS, NPROF, RAD * SUB, cols), jnp.float32),
        ),
        in_specs=vmem_specs(5),
        out_specs=vmem_specs(3),
        compiler_params=grant(16),
        cost_estimate=estimate(1 << 28),
    )(inside, columns, weights, science, table)
    part, late_images = pl.pallas_call(
        second,
        out_shape=(normal, jax.ShapeDtypeStruct((STEPS, RAD, STACK, cols), jnp.float32)),
        in_specs=vmem_specs(6),
        out_specs=vmem_specs(2),
        compiler_params=grant(16),
        cost_estimate=estimate(1 << 28),
    )(across, weights, science, table, part, partial)

    parts, group = [part], 1
    while group < patches:
        if group > 1:
            parts = [sum(parts[1:], parts[0])]
        size = min(4, patches // group)
        for hop in range(group, size * group, group):
            pairs = [(i, i ^ hop) for i in range(patches)]
            parts.append(lax.ppermute(parts[0], "patch", pairs))
        group *= size

    def solve(*refs):
        solve_kernel(rows, cols, len(parts), *refs)

    return pl.pallas_call(
        solve,
        out_shape=held,
        in_specs=vmem_specs(len(parts) + 3),
        out_specs=pl.BlockSpec(memory_space=pl.ANY),
        scratch_shapes=[
            pltpu.VMEM(held.shape, held.dtype),
            pltpu.SemaphoreType.DMA((STEPS * PIECES,)),
        ],
        compiler_params=grant(16),
    )(*parts, scale, early_images, late_images)


def solution(mesh):
    return jax.shard_map(
        shards,
        mesh=mesh,
        in_specs=(
            P("visit", None, "patch", None),
            P(),
            P(None, "visit", "patch", None),
            P(None, "visit", "patch", None),
            P(None, "visit", "patch", None),
        ),
        out_specs=P(None, "visit", "patch", None),
        check_vma=False,
    )
```

```python
import jax
import jax.numpy as jnp
import numpy as np
from jax import lax
from jax.experimental import pallas as pl
from jax.experimental.pallas import tpu as pltpu
from jax.sharding import PartitionSpec as P

NPROF = 5
RAD = 10
STEPS = 2
SUB = 8
LANE = 128

GROUPS = NPROF - 1
STACK = GROUPS * SUB
SPARE = SUB - NPROF
SCI_ROW = 2 * SUB + NPROF
SPOTS = [i * SUB + j for i in range(GROUPS) for j in range(NPROF)]
SPOTS += [(j // SPARE) * SUB + NPROF + j % SPARE for j in range(NPROF)]

PIVOTS = 9

PIECES = 2

FIRST_CHUNK, SECOND_CHUNK = 2 * LANE, 4 * LANE

ridge = 1.0


def profile_table():
    offsets = np.arange(-RAD, RAD + 1) * 1.0
    recipe = [(1.0, 0), (1.5, 1), (2.0, 2), (3.0, 0), (4.0, 1)]
    profiles = []
    for spread, degree in recipe[:NPROF]:
        profile = offsets**degree * np.exp(-offsets * offsets / (2.0 * spread * spread))
        for earlier in profiles:
            profile = profile - np.dot(earlier, profile) * earlier
        profile = profile / np.sqrt(np.dot(profile, profile))
        profiles.append(profile)
    return np.stack(profiles)


PARITY = [0, 1, 0, 0, 1]


def split_bf16(x, parts):
    pieces = []
    for _ in range(parts - 1):
        piece = x.astype(jnp.bfloat16).astype(jnp.float32)
        pieces.append(piece)
        x = x - piece
    return pieces + [x]


EXTRA = RAD % SUB
SLOTS = SUB // EXTRA


def vertical_table(rows):
    profiles = profile_table()
    near = RAD - EXTRA
    blank = [None] * (SUB - EXTRA)
    own = list(range(rows))
    above = [list(range(-near, 0)), list(range(-RAD, -near)) + blank]
    below = [list(range(rows, rows + near)), list(range(rows + near, rows + RAD)) + blank]
    both = []
    for inside, across, shift in ((below, above, RAD), (above, below, 0)):
        order = [(k + shift) % rows for k in range(rows)]
        joined = []
        for outputs, blocks in ((order, [own] + inside), (order[rows - RAD :], across)):
            tables = []
            for block in blocks:
                table = np.zeros((len(outputs) * SUB, len(block)), np.float32)
                for n, r in enumerate(outputs):
                    for j in range(NPROF):
                        for e, offset in enumerate(block):
                            if offset is not None and abs(offset - r) <= RAD:
                                table[n * SUB + j, e] = profiles[j, offset - r + RAD]
                hi = table.astype(jnp.bfloat16).astype(np.float32)
                mid = (table - hi).astype(jnp.bfloat16).astype(np.float32)
                low = table - hi - mid
                tables += [hi, hi, mid, hi, mid, low]
            joined.append(np.concatenate(tables, axis=1))
        width = max(table.shape[1] for table in joined)
        joined = [np.pad(table, ((0, 0), (0, width - table.shape[1]))) for table in joined]
        both.append(np.concatenate(joined, axis=0))
    return jnp.asarray(np.stack(both), jnp.bfloat16)


def patch_parity():
    return lax.rem(lax.axis_index("patch"), 2)


def six_products(hi, mid, low):
    return [hi, mid, hi, low, mid, hi]


def vmem_specs(count):
    return [pl.BlockSpec(memory_space=pltpu.VMEM)] * count


def grant(mebibytes):
    return pltpu.CompilerParams(vmem_limit_bytes=mebibytes * 1024 * 1024)


def estimate(operations):
    return pl.CostEstimate(flops=operations, bytes_accessed=1024 * 1024, transcendentals=0)


def pick_kernel(visits, per, owners, science, table, got, out):
    turn = visits - visits // 2 - 2 * (1 - patch_parity())
    for s in range(STEPS):
        place = lax.rem(owners[s] + turn, jnp.full((SUB, LANE), visits))
        for n in range(per):
            chosen = got[n]
            for v in range(1, visits):
                chosen = jnp.where(place == v, got[v * per + n], chosen)
            for v in range(visits):
                out[v, s, n] = chosen


def exchange(blocks):
    visits, patches = lax.axis_size("visit"), lax.axis_size("patch")
    groups = [
        [(n + visits // 2 + 2 * (1 - p % 2)) % visits * patches + p for n in range(visits)]
        for p in range(patches)
    ]
    return lax.all_to_all(
        blocks, ("visit", "patch"), 0, 0, axis_index_groups=groups, tiled=True
    )


def choose_owned(own, owners, science, table):
    visits = lax.axis_size("visit")
    shape = own.shape
    rows, cols = shape[-2:]
    tiles = own.reshape(shape[0], rows // SUB, SUB, cols // LANE, LANE)
    tiles = jnp.transpose(tiles, (0, 1, 3, 2, 4)).reshape(-1, SUB, LANE)
    per = tiles.shape[0] // visits
    got = exchange(tiles)

    def pick(*refs):
        pick_kernel(visits, per, *refs)

    return pl.pallas_call(
        pick,
        out_shape=jax.ShapeDtypeStruct((visits, STEPS, per, SUB, LANE), jnp.float32),
        in_specs=vmem_specs(1) + [pl.BlockSpec(memory_space=pl.ANY)] * 2 + vmem_specs(1),
        out_specs=vmem_specs(1)[0],
        compiler_params=grant(8),
    )(owners, science, table, got)


def stage_kernel(owners_in, table_in, owners, table):
    owners[...] = owners_in[...]
    table[...] = table_in[...]


def row_cells(ref, s, image, row_tile, shape):
    rows, cols, per = shape
    start = (image * (rows // SUB) + row_tile) * (cols // LANE)
    found = [ref[t // per, s, t % per] for t in range(start, start + cols // LANE)]
    return jnp.concatenate(found, axis=1)


def columns_in_parts(piece):
    profiles = profile_table()
    cols = piece.shape[1]
    width = cols + LANE
    wide = jnp.concatenate([piece, jnp.zeros((SUB, LANE), jnp.float32)], axis=1)
    totals = [piece * float(profiles[i, RAD]) if PARITY[i] == 0 else None for i in range(NPROF)]
    for d in range(1, RAD + 1):
        ahead = pltpu.roll(wide, width - d, 1)[:, :cols]
        behind = pltpu.roll(wide, d, 1)[:, :cols]
        both = (ahead + behind, ahead - behind)
        for i in range(NPROF):
            term = both[PARITY[i]] * float(profiles[i, RAD + d])
            totals[i] = term if totals[i] is None else totals[i] + term
        yield
    return totals


def advance(parts, count=None):
    while count is None or count > 0:
        try:
            next(parts)
        except StopIteration as stop:
            return stop.value
        count = None if count is None else count - 1
    return None


def along_columns(piece):
    return advance(columns_in_parts(piece))


def pass_own_rows(shape, parity, arrived, science_in, signed_var, columns, weights, scale, science):
    rows, cols, _ = shape
    row_tiles = rows // SUB
    sub = lax.broadcasted_iota(jnp.int32, (SUB, cols), 0)

    def put(ref, s, tiles):
        if parity == 0:
            moved = [pltpu.roll(tile, SUB - RAD % SUB, 0) for tile in tiles]
            tiles = []
            for t in range(row_tiles):
                near = (t + RAD // SUB) % row_tiles
                far = (near + 1) % row_tiles
                tiles.append(jnp.where(sub < SUB - RAD % SUB, moved[near], moved[far]))
        for t, tile in enumerate(tiles):
            ref[s, t * SUB : (t + 1) * SUB, :] = tile

    for s in range(STEPS):
        found = [along_columns(row_cells(arrived, s, 0, t, shape)) for t in range(row_tiles)]
        for i in range(NPROF):
            column = jnp.concatenate([piece[i] for piece in found], axis=0)
            for n, piece in enumerate(split_bf16(column, 3)):
                columns[s, i, n] = piece.astype(jnp.bfloat16)
        found = []
        for t in range(row_tiles):
            here = slice(t * SUB, (t + 1) * SUB)
            sci_var = signed_var[s, 0, here, :]
            usable = jnp.where(sci_var > 0.0, 1.0, 0.0)
            noise_var = jnp.abs(sci_var) + row_cells(arrived, s, 1, t, shape)
            found.append(usable / noise_var)
            scale[s, here, :] = usable * lax.rsqrt(noise_var)
        put(weights, s, found)
        put(science, s, [science_in[s, 0, t * SUB : (t + 1) * SUB, :] for t in range(row_tiles)])


def pack_kernel(shape, arrived, science, signed_var, across, inside, *own):
    rows, cols, _ = shape
    last = rows // SUB - 1
    col_tiles = cols // LANE
    odd = jnp.full((SUB, LANE), patch_parity()) == 1
    slot = lax.broadcasted_iota(jnp.int32, (SUB, LANE), 0) // EXTRA
    for s in range(STEPS):
        cells = [row_cells(arrived, s, 0, t, shape) for t in (0, 1, last - 1, last)]
        for group in range(col_tiles // SLOTS):
            tail, head = None, None
            for q in range(SLOTS):
                c = group * SLOTS + q
                there = slice(c * LANE, (c + 1) * LANE)
                first, second, before, final = (cell[:, there] for cell in cells)
                across[s, c] = jnp.where(odd, final, first)
                inside[s, c] = jnp.where(odd, first, final)
                low = pltpu.roll(before, (q + 1) * EXTRA, 0)
                high = pltpu.roll(second, q * EXTRA, 0)
                tail = low if tail is None else jnp.where(slot == q, low, tail)
                head = high if head is None else jnp.where(slot == q, high, head)
            across[s, col_tiles + group] = jnp.where(odd, tail, head)
            inside[s, col_tiles + group] = jnp.where(odd, head, tail)

    @pl.when(patch_parity() == 1)
    def _():
        pass_own_rows(shape, 1, arrived, science, signed_var, *own)


def own_kernel(shape, arrived, science, signed_var, *refs):
    @pl.when(patch_parity() == 0)
    def _():
        pass_own_rows(shape, 0, arrived, science, signed_var, *refs[len(refs) // 2 :])


def near_columns(halo, s, cols):
    return columns_in_parts(jnp.concatenate([halo[s, c] for c in range(cols // LANE)], axis=1))


def extra_columns(halo, cols):
    sub = lax.broadcasted_iota(jnp.int32, (SUB, LANE), 0)
    col_tiles = cols // LANE
    extra = []
    for c in range(col_tiles):
        found = None
        for s in range(STEPS):
            moved = pltpu.roll(
                halo[s, col_tiles + c // SLOTS], (SUB + (s - c % SLOTS) * EXTRA) % SUB, 0
            )
            found = moved if found is None else jnp.where(sub < s * EXTRA, found, moved)
        extra.append(found)
    extra = along_columns(jnp.concatenate(extra, axis=1))
    return [[pltpu.roll(x, SUB - s * EXTRA, 0) if s else x for x in extra] for s in range(STEPS)]


def split_tile(tile):
    return jnp.concatenate(six_products(*split_bf16(tile, 3)), axis=0).astype(jnp.bfloat16)


def fit_rows(s, first, count, there, images, weights, science, stack):
    sub = lax.broadcasted_iota(jnp.int32, (SUB, there.stop - there.start), 0)
    total = None
    for n in range(count):
        k = first + n
        here = slice(n * SUB, (n + 1) * SUB)
        last = images[GROUPS][here, :]
        groups = []
        for i in range(GROUPS):
            found = images[i][here, :]
            if i < 2:
                turn = (NPROF - i * SPARE) % SUB
                found = jnp.where(sub < NPROF, found, pltpu.roll(last, turn, 0))
            elif i == 2:
                found = jnp.where(sub == NPROF, science[s, k : k + 1, there], found)
            stack[s, n, i * SUB : (i + 1) * SUB, there] = found
            groups.append(found)
        found = jnp.concatenate(groups, axis=0)
        hi = found.astype(jnp.bfloat16)
        mid = (found - hi.astype(jnp.float32)).astype(jnp.bfloat16)
        rounded = (found * weights[s, k : k + 1, there]).astype(jnp.bfloat16)
        product = lax.dot_general(
            jnp.concatenate([rounded, rounded], axis=1),
            jnp.concatenate([hi, mid], axis=1),
            (((1,), (1,)), ((), ())),
            preferred_element_type=jnp.float32,
        )
        total = product if total is None else total + product
    return total


def fit_chunks(halo, cols, chunk, first, count, vertical, weights, science, stack):
    extra = extra_columns(halo, cols)
    near = advance(near_columns(halo, 0, cols))
    starts = range(0, cols, chunk)
    items = [(s, slice(start, start + chunk)) for s in range(STEPS) for start in starts]
    images = vertical(0, items[0][1], near, extra[0])
    totals = [None] * STEPS
    coming = None
    for n, (s, there) in enumerate(items):
        following = items[n + 1] if n + 1 < len(items) else None
        if following is not None:
            if s + 1 < STEPS:
                if coming is None:
                    coming, found = near_columns(halo, s + 1, cols), None
                share = None if following[0] != s else -(-RAD // (len(starts) - 1))
                found = advance(coming, share) if found is None else found
            if following[0] != s:
                near, coming = found, None
            upcoming = vertical(*following, near, extra[following[0]])
        total = fit_rows(s, first, count, there, images, weights, science, stack)
        totals[s] = total if totals[s] is None else totals[s] + total
        images = upcoming if following is not None else None
    sides = []
    for total in totals:
        sides.append(total)
        sides.append(jnp.zeros((STACK, LANE // STEPS - STACK), jnp.float32))
    return jnp.concatenate(sides, axis=1)


def first_kernel(shape, inside, own, weights, science, table, normal, stack, partial):
    rows, cols, _ = shape
    early = rows - RAD

    def vertical(s, there, near, extra):
        images = []
        for i in range(NPROF):
            spread = six_products(*(own[s, i, n, :, there] for n in range(3)))
            spread += [split_tile(near[i][:, there]), split_tile(extra[i][:, there])]
            image = jnp.dot(
                table[patch_parity(), : rows * SUB, :],
                jnp.concatenate(spread, axis=0),
                preferred_element_type=jnp.float32,
            )
            images.append(image[: early * SUB, :])
            partial[s, i, :, there] = image[early * SUB :, :]
        return images

    normal[...] = fit_chunks(inside, cols, FIRST_CHUNK, 0, early, vertical, weights, science, stack)


def second_kernel(shape, across, weights, science, table, before, partial, normal, stack):
    rows, cols, _ = shape

    def vertical(s, there, near, extra):
        images = []
        for i in range(NPROF):
            spread = [split_tile(near[i][:, there]), split_tile(extra[i][:, there])]
            spread = jnp.concatenate(spread, axis=0)
            image = jnp.dot(
                table[patch_parity(), rows * SUB :, : spread.shape[0]],
                spread,
                preferred_element_type=jnp.float32,
            )
            images.append(partial[s, i, :, there] + image)
        return images

    found = fit_chunks(
        across, cols, SECOND_CHUNK, rows - RAD, RAD, vertical, weights, science, stack
    )
    normal[...] = before[...] + found


def solve_both(blocks):
    half = LANE // STEPS
    sub = lax.broadcasted_iota(jnp.int32, (SUB, LANE), 0)
    lane = lax.broadcasted_iota(jnp.int32, (SUB, LANE), 1)

    def spread(k):
        return [
            jnp.where(lane < half, block[:, k : k + 1], block[:, half + k : half + k + 1])
            for block in blocks
        ]

    def entry(column, k):
        row = column[k // SUB][k % SUB : k % SUB + 1, :]
        return jnp.broadcast_to(row, (SUB, LANE))

    for start in range(0, len(SPOTS), PIVOTS):
        spots = SPOTS[start : start + PIVOTS]
        columns = [spread(k) for k in spots]
        inner = [[entry(column, k) for column in columns] for k in spots]
        rows = [entry(blocks, k) for k in spots]
        for t in range(len(spots)):
            inverse = 1.0 / inner[t][t]
            inner[t] = [x * inverse for x in inner[t]]
            rows[t] = rows[t] * inverse
            for n in range(len(spots)):
                if n != t:
                    factor = inner[n][t]
                    inner[n] = [x - factor * y for x, y in zip(inner[n], inner[t])]
                    rows[n] = rows[n] - factor * rows[t]
        updated = []
        for i, block in enumerate(blocks):
            terms = [column[i] * row for column, row in zip(columns, rows)]
            while len(terms) > 1:
                terms = [sum(terms[n : n + 2][1:], terms[n]) for n in range(0, len(terms), 2)]
            block = block - terms[0]
            for k, row in zip(spots, rows):
                if k // SUB == i:
                    block = jnp.where(sub == k % SUB, row, block)
            updated.append(block)
        blocks = updated
    return blocks


def fold_rows(found):
    sub = lax.broadcasted_iota(jnp.int32, found[0].shape, 0)
    hop = SUB // 2
    while hop:
        upper = (sub & hop) != 0
        count = len(found) // 2
        joined = []
        for low, high in zip(found[:count], found[count:]):
            kept = jnp.where(upper, high, low)
            if 2 * hop == SUB:
                moved = pltpu.roll(jnp.where(upper, low, high), hop, 0)
            else:
                moved = jnp.where(
                    upper, pltpu.roll(high, hop, 0), pltpu.roll(low, SUB - hop, 0)
                )
            joined.append(kept + moved)
        found = joined
        hop //= 2
    return found[0]


def solve_kernel(rows, cols, count, *refs):
    parts, (scale, early, late, out, held, sems) = refs[:count], refs[count:]
    copies = []
    odd = jnp.full((SUB, LANE), patch_parity()) == 1
    turn = rows - RAD
    half = LANE // STEPS
    sub = lax.broadcasted_iota(jnp.int32, (SUB, LANE), 0)
    lane = lax.broadcasted_iota(jnp.int32, (SUB, LANE), 1)
    blocks = []
    for start in range(0, STACK, SUB):
        block = jnp.where(lax.rem(lane, half) == sub + start, ridge, 0.0)
        for part in parts:
            block = block + part[start : start + SUB, :]
        blocks.append(block)
    solved = solve_both(blocks)
    for s in range(STEPS):
        factors = []
        for i in range(GROUPS):
            spot = s * half + SCI_ROW
            factor = jnp.broadcast_to(solved[i][:, spot : spot + 1], (SUB, LANE))
            used = [k % SUB for k in SPOTS if k // SUB == i]
            if len(used) < SUB:
                factor = jnp.where(sub < len(used), factor, 0.0)
            if i == SCI_ROW // SUB:
                factor = jnp.where(sub == SCI_ROW % SUB, -1.0, factor)
            factors.append(factor)
        for c in range(cols // LANE):
            there = slice(c * LANE, (c + 1) * LANE)
            found = []
            for k in range(rows):
                source, n = (early, k) if k < turn else (late, k - turn)
                total = source[s, n, 0:SUB, there] * factors[0]
                for i in range(1, GROUPS):
                    total = total + source[s, n, i * SUB : (i + 1) * SUB, there] * factors[i]
                found.append(total)
            tiles = [fold_rows(found[k : k + SUB]) for k in range(0, rows, SUB)]
            moved = [pltpu.roll(tile, (SUB - turn) % SUB, 0) for tile in tiles]
            for t, tile in enumerate(tiles):
                after = (t + turn // SUB) % len(tiles)
                ahead = (after + 1) % len(tiles)
                turned = jnp.where(sub < SUB - turn % SUB, moved[after], moved[ahead])
                here = slice(t * SUB, (t + 1) * SUB)
                left = jnp.where(odd, tile, turned)
                held[s, 0, here, there] = -left * scale[s, here, there]
            if there.stop % (cols // PIECES) == 0:
                whole = (s, slice(None), slice(None), pl.ds(there.stop - cols // PIECES, cols // PIECES))
                copy = pltpu.make_async_copy(held.at[whole], out.at[whole], sems.at[len(copies)])
                copy.start()
                copies.append(copy)
    for copy in copies:
        copy.wait()


def shards(templates, owners, science, sci_var, bad_pixels):
    rows, cols = templates.shape[-2:]
    image = jax.ShapeDtypeStruct((STEPS, rows, cols), jnp.float32)
    held = jax.ShapeDtypeStruct(science.shape, jnp.float32)
    bad = bad_pixels != 0
    science = jnp.where(bad, 0.0, science)
    signed_var = jnp.where(bad, -sci_var, sci_var)
    table = vertical_table(rows)
    owners = jnp.broadcast_to(owners[:, None, None], (STEPS, SUB, LANE))
    owners, table = pl.pallas_call(
        stage_kernel,
        out_shape=[jax.ShapeDtypeStruct(x.shape, x.dtype) for x in (owners, table)],
        in_specs=vmem_specs(2),
        out_specs=vmem_specs(2),
        compiler_params=grant(8),
        cost_estimate=estimate(1 << 20),
    )(owners, table)
    chosen = choose_owned(templates[0], owners, science, table)
    arrived = exchange(chosen)
    visits, per = arrived.shape[0], arrived.shape[2]
    shape = (rows, cols, per)

    own_shapes = (
        jax.ShapeDtypeStruct((STEPS, NPROF, 3, rows, cols), jnp.bfloat16),
        image,
        image,
        image,
    )

    def pack(*refs):
        pack_kernel(shape, *refs)

    tiles = cols // LANE
    packed = jax.ShapeDtypeStruct((STEPS, tiles + tiles // SLOTS, SUB, LANE), jnp.float32)
    across, inside, *own = pl.pallas_call(
        pack,
        out_shape=(packed, packed) + own_shapes,
        in_specs=vmem_specs(3),
        out_specs=vmem_specs(6),
        compiler_params=grant(8),
    )(arrived, science, signed_var)
    patches = lax.axis_size("patch")
    swaps = [(i, i + 1) for i in range(1, patches - 1, 2)]
    across = lax.ppermute(across, "patch", swaps + [(b, a) for a, b in swaps])
    inside = lax.ppermute(inside, "patch", [(i, i ^ 1) for i in range(patches)])

    def own_rows(*refs):
        own_kernel(shape, *refs)

    columns, weights, scale, science = pl.pallas_call(
        own_rows,
        out_shape=own_shapes,
        in_specs=vmem_specs(7),
        out_specs=vmem_specs(4),
        input_output_aliases={3: 0, 4: 1, 5: 2, 6: 3},
        compiler_params=grant(8),
        cost_estimate=estimate(1 << 28),
    )(arrived, science, signed_var, *own)

    def first(*refs):
        first_kernel(shape, *refs)

    def second(*refs):
        second_kernel(shape, *refs)

    normal = jax.ShapeDtypeStruct((STACK, LANE), jnp.float32)
    part, early_images, partial = pl.pallas_call(
        first,
        out_shape=(
            normal,
            jax.ShapeDtypeStruct((STEPS, rows - RAD, STACK, cols), jnp.float32),
            jax.ShapeDtypeStruct((STEPS, NPROF, RAD * SUB, cols), jnp.float32),
        ),
        in_specs=vmem_specs(5),
        out_specs=vmem_specs(3),
        compiler_params=grant(16),
        cost_estimate=estimate(1 << 28),
    )(inside, columns, weights, science, table)
    part, late_images = pl.pallas_call(
        second,
        out_shape=(normal, jax.ShapeDtypeStruct((STEPS, RAD, STACK, cols), jnp.float32)),
        in_specs=vmem_specs(6),
        out_specs=vmem_specs(2),
        compiler_params=grant(16),
        cost_estimate=estimate(1 << 28),
    )(across, weights, science, table, part, partial)

    parts, group = [part], 1
    while group < patches:
        if group > 1:
            parts = [sum(parts[1:], parts[0])]
        size = min(4, patches // group)
        for hop in range(group, size * group, group):
            pairs = [(i, i ^ hop) for i in range(patches)]
            parts.append(lax.ppermute(parts[0], "patch", pairs))
        group *= size

    def solve(*refs):
        solve_kernel(rows, cols, len(parts), *refs)

    return pl.pallas_call(
        solve,
        out_shape=held,
        in_specs=vmem_specs(len(parts) + 3),
        out_specs=pl.BlockSpec(memory_space=pl.ANY),
        scratch_shapes=[
            pltpu.VMEM(held.shape, held.dtype),
            pltpu.SemaphoreType.DMA((STEPS * PIECES,)),
        ],
        compiler_params=grant(16),
    )(*parts, scale, early_images, late_images)


def solution(mesh):
    return jax.shard_map(
        shards,
        mesh=mesh,
        in_specs=(
            P("visit", None, "patch", None),
            P(),
            P(None, "visit", "patch", None),
            P(None, "visit", "patch", None),
            P(None, "visit", "patch", None),
        ),
        out_specs=P(None, "visit", "patch", None),
        check_vma=False,
    )
```
